32 devices in a mesh: batch: 4 (over z), ctx: 2 (over y), head: 4 (over x, core).
Axes of the slice: x: 2, y: 2, z: 4, core: 2. Of those that a mesh axis runs over, the one named last changes fastest.
Arguments:
- tokens: bfloat16 [4, 1024, 640], P('batch', ('ctx', 'head')), may hold values from -6 to 6
- attn_in_gain: float32 [640], replicated, may hold values from 0.25 to 1.75
- query_weight: bfloat16 [640, 1024], P(None, ('batch', 'ctx')), may hold values from -0.25 to 0.25
- key_weight: bfloat16 [640, 256], P(None, ('batch', 'ctx')), may hold values from -0.25 to 0.25
- value_weight: bfloat16 [640, 256], P(None, ('batch', 'ctx')), may hold values from -0.25 to 0.25
- query_gain: float32 [256], replicated, may hold values from 0.25 to 1.75
- key_gain: float32 [256], replicated, may hold values from 0.25 to 1.75
- out_weight: bfloat16 [1024, 640], P(('batch', 'ctx')), may hold values from -0.1875 to 0.1875
- attn_out_gain: float32 [640], replicated, may hold values from 0.25 to 1.75
- ffn_in_gain: float32 [640], replicated, may hold values from 0.25 to 1.75
- gate_weight: bfloat16 [640, 2048], P(None, ('batch', 'ctx')), may hold values from -0.25 to 0.25
- up_weight: bfloat16 [640, 2048], P(None, ('batch', 'ctx')), may hold values from -0.25 to 0.25
- down_weight: bfloat16 [2048, 640], P(('batch', 'ctx')), may hold values from -0.125 to 0.125
- ffn_out_gain: float32 [640], replicated, may hold values from 0.25 to 1.75
- cotangent: bfloat16 [4, 1024, 640], P('batch', ('ctx', 'head')), may hold values from -6 to 6
Outputs:
- block_out: bfloat16 [4, 1024, 640], P('batch', ('ctx', 'head'))
- tokens_grad: float32 [4, 1024, 640], P('batch', ('ctx', 'head'))
- attn_in_gain_grad: float32 [640], replicated
- query_weight_grad: float32 [640, 1024], P(None, ('batch', 'ctx'))
- key_weight_grad: float32 [640, 256], P(None, ('batch', 'ctx'))
- value_weight_grad: float32 [640, 256], P(None, ('batch', 'ctx'))
- query_gain_grad: float32 [256], replicated
- key_gain_grad: float32 [256], replicated
- out_weight_grad: float32 [1024, 640], P(('batch', 'ctx'))
- attn_out_gain_grad: float32 [640], replicated
- ffn_in_gain_grad: float32 [640], replicated
- gate_weight_grad: float32 [640, 2048], P(None, ('batch', 'ctx'))
- up_weight_grad: float32 [640, 2048], P(None, ('batch', 'ctx'))
- down_weight_grad: float32 [2048, 640], P(('batch', 'ctx'))
- ffn_out_gain_grad: float32 [640], replicated
The draws below stay inside these ranges and needn't reach their ends.
All inputs are finite; a program needn't handle non-finite values.
Results may differ from the reference program's by a relative error of at most 0.02.
Values may be sent and summed in bfloat16 or wider, within the bound.
A program may use at most 128 MiB of HBM per device.

```python
import math
import jax
import jax.numpy as jnp
from jax import lax

D = 640
NH = 4
HD = 256
FF = 2048
LEN = 1024
SEQS = 4


def levels(own_key, shape, pieces, smallest, high):
    level = 1.0
    for axis_at, blocks in pieces:
        heights = jax.random.uniform(jax.random.fold_in(jax.random.fold_in(own_key, 6), axis_at), (blocks,), jnp.float32, smallest / len(pieces), high / len(pieces))
        level = level * jnp.repeat(jnp.exp(heights), shape[axis_at] // blocks).reshape((-1,) + (1,) * (len(shape) - 1 - axis_at))
    return level


def gaussian(own_key, extent, scale, reach, pieces=(), held_as=jnp.bfloat16):
    values = jax.random.normal(own_key, extent, jnp.float32) * scale
    if len(pieces) > 0:
        values = levels(own_key, extent, pieces, -0.22, 0.18) * values
    return jnp.clip(values, min=-reach, max=reach).astype(held_as)


def setup_inputs(seed: int = 0) -> dict:
    arg_keys = jax.random.split(jax.random.key(seed), 16)
    return {
        "tokens": gaussian(arg_keys[0], (SEQS, LEN, D), 1.0, 6.0, ((0, 4), (1, 8))),
        "attn_in_gain": jnp.clip(1.0 + 0.15 * jax.random.normal(arg_keys[1], (D,), jnp.float32), 0.25, 1.75),
        "query_weight": gaussian(arg_keys[2], (D, NH * HD), D ** -0.5, 0.25, ((1, 8),)),
        "key_weight": gaussian(arg_keys[3], (D, HD), D ** -0.5, 0.25, ((1, 8),)),
        "value_weight": gaussian(arg_keys[4], (D, HD), D ** -0.5, 0.25, ((1, 8),)),
        "query_gain": jnp.clip(1.0 + 0.15 * jax.random.normal(arg_keys[5], (HD,), jnp.float32), 0.25, 1.75),
        "key_gain": jnp.clip(1.0 + 0.15 * jax.random.normal(arg_keys[6], (HD,), jnp.float32), 0.25, 1.75),
        "out_weight": gaussian(arg_keys[7], (NH * HD, D), (NH * HD) ** -0.5, 0.1875, ((0, 8),)),
        "attn_out_gain": jnp.clip(1.0 + 0.15 * jax.random.normal(arg_keys[8], (D,), jnp.float32), 0.25, 1.75),
        "ffn_in_gain": jnp.clip(1.0 + 0.15 * jax.random.normal(arg_keys[9], (D,), jnp.float32), 0.25, 1.75),
        "gate_weight": gaussian(arg_keys[10], (D, FF), D ** -0.5, 0.25, ((1, 8),)),
        "up_weight": gaussian(arg_keys[11], (D, FF), D ** -0.5, 0.25, ((1, 8),)),
        "down_weight": gaussian(arg_keys[12], (FF, D), FF ** -0.5, 0.125, ((0, 8),)),
        "ffn_out_gain": jnp.clip(1.0 + 0.15 * jax.random.normal(arg_keys[13], (D,), jnp.float32), 0.25, 1.75),
        "cotangent": gaussian(arg_keys[14], (SEQS, LEN, D), 1.0, 6.0, ((0, 4), (1, 8))),
    }


@jax.custom_vjp
def low(v):
    return lax.optimization_barrier(v.astype(jnp.bfloat16)).astype(jnp.float32)

@jax.custom_vjp
def low_back(v):
    return v

def low_keep(v):
    return (low(v), None)

def low_pass(kept, grad):
    return (grad,)

def back_keep(v):
    return (v, None)

def back_low(kept, grad):
    return (low(grad),)
low.defvjp(low_keep, low_pass)
low_back.defvjp(back_keep, back_low)
norm_eps = 1e-06
rope_base = 1000000.0

def matmul(left, right):
    return jnp.dot(left, right, precision=lax.Precision.HIGHEST, preferred_element_type=jnp.float32)

def rms_scale(values, gain):
    return values * lax.rsqrt(lax.optimization_barrier(jnp.mean(values * values, axis=-1, keepdims=True)) + norm_eps) * gain

def angles(positions, size):
    half_size = size // 2
    freq = jnp.exp(jnp.arange(half_size, dtype=jnp.float32) * (-2.0 * math.log(rope_base) / size))
    turned = positions[:, None] * freq[None, :]
    return (jnp.cos(turned), jnp.sin(turned))

def rotate(values, cosine, sine):
    half_size = values.shape[-1] // 2
    first = values[..., :half_size]
    second = values[..., half_size:]
    return jnp.concatenate([first * cosine - second * sine, second * cosine + first * sine], axis=-1)

def geglu(gate_pre, up_pre):
    return jax.nn.gelu(gate_pre, approximate=True) * up_pre

def attend(queries, key_rows, value_rows):
    length = key_rows.shape[0]
    block = min(512, length)
    count = length // block
    scale = queries.shape[-1] ** (-0.5)
    key_pos = jnp.arange(length, dtype=jnp.int32)

    def one_block(inputs):
        query_block, start = inputs
        scores = low_back(jnp.einsum('qhd,kd->hqk', query_block, key_rows, precision=lax.Precision.HIGHEST) * scale)
        query_pos = start + jnp.arange(block, dtype=jnp.int32)
        scores = jnp.where(key_pos[None, None, :] <= query_pos[None, :, None], scores, -jnp.inf)
        probs = low(jnp.exp(scores - jax.nn.logsumexp(scores, axis=-1, keepdims=True)))
        return jnp.einsum('hqk,kd->qhd', probs, value_rows, precision=lax.Precision.HIGHEST)
    blocks = queries.reshape(count, block, queries.shape[1], queries.shape[2])
    starts = jnp.arange(count, dtype=jnp.int32) * block
    return lax.map(jax.checkpoint(one_block), (blocks, starts)).reshape(queries.shape)

def layer(inputs, attn_in_gain, query_weight, key_weight, value_weight, query_gain, key_gain, out_weight, attn_out_gain, ffn_in_gain, gate_weight, up_weight, down_weight, ffn_out_gain):
    length = inputs.shape[0]
    head_dim = key_gain.shape[0]
    heads = query_weight.shape[1] // head_dim
    positions = jnp.arange(length, dtype=jnp.float32)
    cosine, sine = angles(positions, head_dim)
    normed_in = low(rms_scale(inputs, attn_in_gain))
    query_raw = low_back(matmul(normed_in, query_weight)).reshape(length, heads, head_dim)
    key_raw = low_back(matmul(normed_in, key_weight))
    value_low = low_back(low(matmul(normed_in, value_weight)))
    query_low = low_back(low(rotate(rms_scale(query_raw, query_gain), cosine[:, None, :], sine[:, None, :])))
    key_low = low(rotate(rms_scale(key_raw, key_gain), cosine, sine))
    attended = attend(query_low, key_low, value_low)
    attended_low = low_back(low(attended)).reshape(length, heads * head_dim)
    projected = low_back(matmul(attended_low, out_weight))
    resid = inputs + rms_scale(projected, attn_out_gain)
    normed_ffn = low(rms_scale(resid, ffn_in_gain))
    gate_pre = low_back(matmul(normed_ffn, gate_weight))
    up_pre = low_back(matmul(normed_ffn, up_weight))
    hidden = low(geglu(gate_pre, up_pre))
    mixed = low_back(matmul(hidden, down_weight))
    return resid + rms_scale(mixed, ffn_out_gain)

def reference(tokens, attn_in_gain, query_weight, key_weight, value_weight, query_gain, key_gain, out_weight, attn_out_gain, ffn_in_gain, gate_weight, up_weight, down_weight, ffn_out_gain, cotangent):
    params = tuple((p.astype(jnp.float32) for p in (attn_in_gain, query_weight, key_weight, value_weight, query_gain, key_gain, out_weight, attn_out_gain, ffn_in_gain, gate_weight, up_weight, down_weight, ffn_out_gain)))

    def forward(inputs, weights):

        def one_seq(carry, sequence):
            return (carry, layer(sequence, *weights))
        return lax.scan(one_seq, jnp.zeros((), jnp.float32), inputs)[1]
    outputs, pull = jax.vjp(forward, tokens.astype(jnp.float32), params)
    inputs_grad, grads = pull(cotangent.astype(jnp.float32))
    return (outputs.astype(jnp.bfloat16), inputs_grad, grads[0], grads[1], grads[2], grads[3], grads[4], grads[5], grads[6], grads[7], grads[8], grads[9], grads[10], grads[11], grads[12])
```

```python
import functools
import math

import jax
import jax.numpy as jnp
from jax import lax
from jax.experimental import pallas as pl
from jax.experimental.pallas import tpu as pltpu
from jax.sharding import PartitionSpec as P

norm_eps = 1e-06
rope_base = 1000000.0


def rms_scale(values, gain):
    return values * lax.rsqrt(jnp.mean(values * values, axis=-1, keepdims=True) + norm_eps) * gain


def angles(positions, size):
    half_size = size // 2
    freq = jnp.exp(jnp.arange(half_size, dtype=jnp.float32) * (-2.0 * math.log(rope_base) / size))
    turned = positions[:, None] * freq[None, :]
    return (jnp.cos(turned), jnp.sin(turned))


def rotate(values, cosine, sine):
    half_size = values.shape[-1] // 2
    first = values[..., :half_size]
    second = values[..., half_size:]
    return jnp.concatenate(
        [first * cosine - second * sine, second * cosine + first * sine], axis=-1
    )


def geglu(gate_pre, up_pre):
    return jax.nn.gelu(gate_pre, approximate=True) * up_pre


def contract_rows(left, right):
    return lax.dot_general(
        left, right, (((0,), (0,)), ((), ())), preferred_element_type=jnp.float32
    )


def contract_cols(left, right):
    return lax.dot_general(
        left, right, (((1,), (1,)), ((), ())), preferred_element_type=jnp.float32
    )


vmem_limit = 52 * 1024 * 1024


def greet(axes):
    barrier = pltpu.get_barrier_semaphore()
    count = 0
    for axis in axes:
        size = lax.axis_size(axis)
        me = lax.axis_index(axis)
        for step in range(1, size):
            pl.semaphore_signal(
                barrier,
                inc=1,
                device_id={axis: lax.rem(me + step, size)},
                device_id_type=pl.DeviceIdType.MESH,
            )
            count += 1
    pl.semaphore_wait(barrier, count)


def send(source, target, send_sem, recv_sem, axis, index):
    copy = pltpu.make_async_remote_copy(
        src_ref=source,
        dst_ref=target,
        send_sem=send_sem,
        recv_sem=recv_sem,
        device_id={axis: index},
        device_id_type=pl.DeviceIdType.MESH,
    )
    copy.start()
    return copy


def gather_kernel(first, second, x_ref, out_ref, own_sem, send_a, recv_a, send_b, recv_b):
    size_a, size_b = lax.axis_size(first), lax.axis_size(second)
    at_a, at_b = lax.axis_index(first), lax.axis_index(second)
    greet((first, second))
    own = out_ref.at[at_a, at_b]
    sent_a, sent_b = [], []
    for step in range(1, size_a):
        sent_a.append(
            send(x_ref, own, send_a.at[step - 1], recv_a.at[step - 1], first,
                 lax.rem(at_a + step, size_a))
        )
    for turn in range(1, size_b):
        sent_b.append(
            send(x_ref, own, send_b.at[turn - 1, 0], recv_b.at[turn - 1, 0], second,
                 lax.rem(at_b + turn, size_b))
        )
    keep = pltpu.make_async_copy(x_ref, own, own_sem)
    keep.start()
    for step in range(1, size_a):
        sent_a[step - 1].wait_recv()
        slot = out_ref.at[lax.rem(at_a + size_a - step, size_a), at_b]
        for turn in range(1, size_b):
            sent_b.append(
                send(slot, slot, send_b.at[turn - 1, step], recv_b.at[turn - 1, step], second,
                     lax.rem(at_b + turn, size_b))
            )
    for copy in sent_b:
        copy.wait_recv()
    for copy in sent_a + sent_b:
        copy.wait_send()
    keep.wait()


def gather(values, first, second, number):
    size_a, size_b = lax.axis_size(first), lax.axis_size(second)
    dma = pltpu.SemaphoreType.DMA
    return pl.pallas_call(
        functools.partial(gather_kernel, first, second),
        out_shape=jax.ShapeDtypeStruct((size_a, size_b) + values.shape, values.dtype),
        in_specs=[pl.BlockSpec(memory_space=pl.ANY)],
        out_specs=pl.BlockSpec(memory_space=pl.ANY),
        scratch_shapes=[
            dma,
            dma((size_a - 1,)),
            dma((size_a - 1,)),
            dma((size_b - 1, size_a)),
            dma((size_b - 1, size_a)),
        ],
        compiler_params=pltpu.CompilerParams(
            collective_id=number, has_side_effects=True, vmem_limit_bytes=vmem_limit
        ),
        name="gather_" + first + "_" + second,
    )(values)


def scatter_kernel(
    first, second, x_ref, out_ref, held_b, part, held_a, send_a, recv_a, send_b, recv_b
):
    size_a, size_b = lax.axis_size(first), lax.axis_size(second)
    at_a, at_b = lax.axis_index(first), lax.axis_index(second)
    greet((first, second))
    order = list(range(1, size_a)) + [0]
    sent_a, sent_b = {}, {}
    for step in order:
        goal = lax.rem(at_a + step, size_a)
        for turn in range(1, size_b):
            other = lax.rem(at_b + turn, size_b)
            sent_b[turn, step] = send(
                x_ref.at[goal, other], held_b.at[turn - 1, step],
                send_b.at[turn - 1, step], recv_b.at[turn - 1, step], second, other,
            )
    for step in order:
        goal = lax.rem(at_a + step, size_a)
        total = x_ref[goal, at_b].astype(jnp.float32)
        for turn in range(1, size_b):
            sent_b[turn, step].wait_recv()
            total += held_b[turn - 1, step].astype(jnp.float32)
        if step > 0:
            part[step - 1] = total.astype(part.dtype)
            sent_a[step] = send(
                part.at[step - 1], held_a.at[step - 1],
                send_a.at[step - 1], recv_a.at[step - 1], first, goal,
            )
        else:
            for back in range(1, size_a):
                sent_a[back].wait_recv()
                total += held_a[back - 1].astype(jnp.float32)
            out_ref[...] = total.astype(out_ref.dtype)
    for copy in list(sent_a.values()) + list(sent_b.values()):
        copy.wait_send()


def scatter_sum(values, first, second, number, dtype=jnp.float32):
    size_a, size_b = lax.axis_size(first), lax.axis_size(second)
    block = values.shape[2:]
    dma = pltpu.SemaphoreType.DMA
    return pl.pallas_call(
        functools.partial(scatter_kernel, first, second),
        out_shape=jax.ShapeDtypeStruct(block, dtype),
        in_specs=[pl.BlockSpec(memory_space=pltpu.VMEM)],
        out_specs=pl.BlockSpec(memory_space=pltpu.VMEM),
        scratch_shapes=[
            pltpu.VMEM((size_b - 1, size_a) + block, values.dtype),
            pltpu.VMEM((size_a - 1,) + block, values.dtype),
            pltpu.VMEM((size_a - 1,) + block, values.dtype),
            dma((size_a - 1,)),
            dma((size_a - 1,)),
            dma((size_b - 1, size_a)),
            dma((size_b - 1, size_a)),
        ],
        compiler_params=pltpu.CompilerParams(
            collective_id=number, has_side_effects=True, vmem_limit_bytes=vmem_limit
        ),
        name="scatter_" + first + "_" + second,
    )(values)


def total_kernel(axis, x_ref, out_ref, held, send_a, recv_a, send_b, recv_b):
    size = lax.axis_size(axis)
    me = lax.axis_index(axis)
    greet((axis,))
    sent = []
    for step in range(1, size):
        other = lax.rem(me + step, size)
        sent.append(
            send(x_ref.at[other], held.at[step - 1], send_a.at[step - 1], recv_a.at[step - 1],
                 axis, other)
        )
    total = x_ref[me].astype(jnp.float32)
    for step in range(1, size):
        sent[step - 1].wait_recv()
        total += held[step - 1].astype(jnp.float32)
    out_ref[me] = total.astype(out_ref.dtype)
    again = []
    for step in range(1, size):
        again.append(
            send(out_ref.at[me], out_ref.at[me], send_b.at[step - 1], recv_b.at[step - 1],
                 axis, lax.rem(me + step, size))
        )
    for copy in again:
        copy.wait_recv()
    for copy in sent + again:
        copy.wait_send()


def total_over(values, axis, number):
    size = lax.axis_size(axis)
    dma = pltpu.SemaphoreType.DMA
    return pl.pallas_call(
        functools.partial(total_kernel, axis),
        out_shape=jax.ShapeDtypeStruct(values.shape, values.dtype),
        in_specs=[pl.BlockSpec(memory_space=pltpu.VMEM)],
        out_specs=pl.BlockSpec(memory_space=pltpu.VMEM),
        scratch_shapes=[pltpu.VMEM((size - 1,) + values.shape[1:], values.dtype)]
        + [dma((size - 1,))] * 4,
        compiler_params=pltpu.CompilerParams(
            collective_id=number, has_side_effects=True, vmem_limit_bytes=vmem_limit
        ),
        name="total_" + axis,
    )(values)


def local(
    tokens,
    attn_in_gain,
    query_weight,
    key_weight,
    value_weight,
    query_gain,
    key_gain,
    out_weight,
    attn_out_gain,
    ffn_in_gain,
    gate_weight,
    up_weight,
    down_weight,
    ffn_out_gain,
    cotangent,
):
    low = jnp.bfloat16
    size_b, size_c, size_h = (lax.axis_size(axis) for axis in ("batch", "ctx", "head"))
    ctx_index = lax.axis_index("ctx")
    head_index = lax.axis_index("head")
    tok, width = tokens.shape[1:]
    head_dim = key_gain.shape[0]
    n_q, n_k, n_o = query_weight.shape[1], key_weight.shape[1], out_weight.shape[0]
    shards = size_b * size_c
    heads = n_q * shards // head_dim
    scale = head_dim ** (-0.5)

    packed = jnp.concatenate([query_weight.T, key_weight.T, value_weight.T, out_weight], axis=0)
    full = gather(packed, "batch", "ctx", 0).reshape(shards, packed.shape[0], width)
    full_q = full[:, :n_q].reshape(-1, width)
    full_k = full[:, n_q : n_q + n_k].reshape(-1, width)
    full_v = full[:, n_q + n_k : n_q + 2 * n_k].reshape(-1, width)
    full_o = full[:, n_q + 2 * n_k :].reshape(-1, width)

    inputs = tokens[0].astype(jnp.float32)
    first_pos = (ctx_index * size_h + head_index) * tok
    query_pos = first_pos + jnp.arange(tok, dtype=jnp.int32)
    cosine, sine = angles(query_pos.astype(jnp.float32), head_dim)
    normed_f, pull_in = jax.vjp(rms_scale, inputs, attn_in_gain)
    normed_in = normed_f.astype(low)
    query_raw = contract_cols(normed_in, full_q).reshape(tok, heads, head_dim)
    key_raw = contract_cols(normed_in, full_k)
    value_low = contract_cols(normed_in, full_v).astype(low)

    def query_path(values, gain):
        return rotate(rms_scale(values, gain), cosine[:, None, :], sine[:, None, :])

    def key_path(values, gain):
        return rotate(rms_scale(values, gain), cosine, sine)

    query_rot, pull_query = jax.vjp(query_path, query_raw, query_gain)
    key_rot, pull_key = jax.vjp(key_path, key_raw, key_gain)
    key_low = key_rot.astype(low)
    rows = heads * tok
    query_rows = query_rot.astype(low).transpose(1, 0, 2).reshape(rows, head_dim)
    pairs = gather(jnp.concatenate([key_low, value_low], axis=1), "ctx", "head", 1)
    pairs = pairs.reshape(-1, 2 * head_dim)
    key_rows, value_rows = pairs[:, :head_dim], pairs[:, head_dim:]
    length = key_rows.shape[0]

    scores = contract_cols(query_rows, key_rows) * scale
    key_pos = jnp.arange(length, dtype=jnp.int32)
    row_pos = jnp.tile(query_pos, heads)
    scores = jnp.where(key_pos[None, :] <= row_pos[:, None], scores, -jnp.inf)
    row_max = jnp.max(scores, axis=1, keepdims=True)
    raised = jnp.exp(scores - row_max)
    probs = raised * (1.0 / jnp.sum(raised, axis=1, keepdims=True))
    probs_low = probs.astype(low)
    attended = jnp.dot(probs_low, value_rows, preferred_element_type=jnp.float32)

    def to_tokens(values):
        return values.reshape(heads, tok, head_dim).transpose(1, 0, 2).reshape(tok, -1)

    attended_tok = to_tokens(attended.astype(low))
    projected = jnp.dot(attended_tok, full_o, preferred_element_type=jnp.float32)
    post_attn, pull_aout = jax.vjp(rms_scale, projected, attn_out_gain)
    resid = inputs + post_attn
    normed_ffn_f, pull_fin = jax.vjp(rms_scale, resid, ffn_in_gain)
    group_ffn = gather(normed_ffn_f.astype(low), "batch", "ctx", 2).reshape(-1, width)
    gate_pre = jnp.dot(group_ffn, gate_weight, preferred_element_type=jnp.float32)
    up_pre = jnp.dot(group_ffn, up_weight, preferred_element_type=jnp.float32)
    hidden_f, pull_glu = jax.vjp(geglu, gate_pre, up_pre)
    hidden = hidden_f.astype(low)
    mixed_part = jnp.dot(hidden, down_weight, preferred_element_type=jnp.float32).astype(low)
    mixed = scatter_sum(mixed_part.reshape(size_b, size_c, tok, width), "batch", "ctx", 3)
    post_ffn, pull_fout = jax.vjp(rms_scale, mixed, ffn_out_gain)
    block_out = (resid + post_ffn).astype(low)

    out_grad = cotangent[0].astype(jnp.float32)
    mixed_grad_f, fout_gain_grad = pull_fout(out_grad)
    mixed_grad = gather(mixed_grad_f.astype(low), "batch", "ctx", 4).reshape(-1, width)
    hidden_grad = contract_cols(mixed_grad, down_weight)
    gate_grad_f, up_grad_f = pull_glu(hidden_grad)
    gate_grad = gate_grad_f.astype(low)
    up_grad = up_grad_f.astype(low)
    ffn_part = (contract_cols(gate_grad, gate_weight) + contract_cols(up_grad, up_weight)).astype(
        low
    )
    normed_ffn_grad = scatter_sum(ffn_part.reshape(size_b, size_c, tok, width), "batch", "ctx", 5)
    down_grad = contract_rows(hidden, mixed_grad).astype(low)
    gate_w_grad = contract_rows(gate_grad, group_ffn).astype(low)
    up_w_grad = contract_rows(up_grad, group_ffn).astype(low)
    resid_part, fin_gain_grad = pull_fin(normed_ffn_grad)
    resid_grad = out_grad + resid_part
    projected_grad_f, aout_gain_grad = pull_aout(resid_grad)
    projected_grad = projected_grad_f.astype(low)
    out_w_grad = contract_rows(attended_tok, projected_grad).astype(low)
    attended_grad = contract_cols(projected_grad, full_o).astype(low)
    grad_rows = attended_grad.reshape(tok, heads, head_dim).transpose(1, 0, 2).reshape(rows, head_dim)
    delta = jnp.sum(grad_rows.astype(jnp.float32) * attended, axis=1)

    probs_grad = contract_cols(grad_rows, value_rows)
    score_grad = (probs * (probs_grad - delta[:, None])).astype(low)
    query_low_grad = jnp.dot(score_grad, key_rows, preferred_element_type=jnp.float32) * scale
    key_part = contract_rows(score_grad, query_rows) * scale
    value_part = contract_rows(probs_low, grad_rows)
    pair_part = jnp.concatenate([key_part.astype(low), value_part.astype(low)], axis=1)
    pair_grad = scatter_sum(
        pair_part.reshape(size_c, size_h, tok, 2 * head_dim), "ctx", "head", 6
    )
    key_low_grad, value_grad = pair_grad[:, :head_dim], pair_grad[:, head_dim:].astype(low)
    query_low_grad = to_tokens(query_low_grad.astype(low)).reshape(tok, heads, head_dim)
    query_raw_grad_f, query_gain_grad = pull_query(query_low_grad.astype(jnp.float32))
    key_raw_grad_f, key_gain_grad = pull_key(key_low_grad)
    query_raw_grad = query_raw_grad_f.reshape(tok, heads * head_dim).astype(low)
    key_raw_grad = key_raw_grad_f.astype(low)
    query_w_grad = contract_rows(query_raw_grad, normed_in).astype(low)
    key_w_grad = contract_rows(key_raw_grad, normed_in).astype(low)
    value_w_grad = contract_rows(value_grad, normed_in).astype(low)
    normed_in_grad = (
        jnp.dot(query_raw_grad, full_q, preferred_element_type=jnp.float32)
        + jnp.dot(key_raw_grad, full_k, preferred_element_type=jnp.float32)
        + jnp.dot(value_grad, full_v, preferred_element_type=jnp.float32)
    )
    inputs_part, ain_gain_grad = pull_in(normed_in_grad)
    inputs_grad = resid_grad + inputs_part

    gains = (
        ain_gain_grad,
        query_gain_grad,
        key_gain_grad,
        aout_gain_grad,
        fin_gain_grad,
        fout_gain_grad,
    )
    gain_flat = jnp.concatenate(gains)
    gain_rows = -(-gain_flat.shape[0] // width)
    gain_pad = -(-gain_rows // 16) * 16
    gain_block = jnp.pad(gain_flat, (0, gain_pad * width - gain_flat.shape[0])).astype(low)
    gain_block = jnp.broadcast_to(gain_block.reshape(1, gain_pad, width), (shards, gain_pad, width))
    split = (
        query_w_grad.reshape(shards, n_q, width),
        key_w_grad.reshape(shards, n_k, width),
        value_w_grad.reshape(shards, n_k, width),
        out_w_grad.reshape(shards, n_o, width),
        gain_block,
    )
    grads = jnp.concatenate(split, axis=1)
    depth = grads.shape[1]
    summed = scatter_sum(
        grads.reshape(size_b, size_c, depth, width), "batch", "ctx", 7, low
    )
    stacked = jnp.concatenate([summed, gate_w_grad, up_w_grad, down_grad], axis=0)
    unit = 16 * size_h
    used = stacked.shape[0]
    stacked = jnp.pad(stacked, ((0, -used % unit), (0, 0)))
    done = total_over(stacked.reshape(size_h, -1, width), "head", 8)
    done = done.reshape(-1, width).astype(jnp.float32)

    parts = []
    start = 0
    n_f = gate_weight.shape[1]
    for count in (n_q, n_k, n_k, n_o, gain_pad, n_f, n_f, n_f):
        parts.append(done[start : start + count])
        start += count
    gain_done = parts[4].reshape(-1)
    gain_out = []
    start = 0
    for gain in gains:
        gain_out.append(gain_done[start : start + gain.shape[0]])
        start += gain.shape[0]
    return (
        block_out[None],
        inputs_grad[None],
        gain_out[0],
        parts[0].T,
        parts[1].T,
        parts[2].T,
        gain_out[1],
        gain_out[2],
        parts[3],
        gain_out[3],
        gain_out[4],
        parts[5].T,
        parts[6].T,
        parts[7],
        gain_out[5],
    )


def solution(mesh):
    in_specs = (
        P("batch", ("ctx", "head"), None),
        P(),
        P(None, ("batch", "ctx")),
        P(None, ("batch", "ctx")),
        P(None, ("batch", "ctx")),
        P(),
        P(),
        P(("batch", "ctx"), None),
        P(),
        P(),
        P(None, ("batch", "ctx")),
        P(None, ("batch", "ctx")),
        P(("batch", "ctx"), None),
        P(),
        P("batch", ("ctx", "head"), None),
    )
    out_specs = (
        P("batch", ("ctx", "head"), None),
        P("batch", ("ctx", "head"), None),
        P(),
        P(None, ("batch", "ctx")),
        P(None, ("batch", "ctx")),
        P(None, ("batch", "ctx")),
        P(),
        P(),
        P(("batch", "ctx"), None),
        P(),
        P(),
        P(None, ("batch", "ctx")),
        P(None, ("batch", "ctx")),
        P(("batch", "ctx"), None),
        P(),
    )
    return jax.shard_map(local, mesh=mesh, in_specs=in_specs, out_specs=out_specs, check_vma=False)
```

```python
import functools
import math

import jax
import jax.numpy as jnp
from jax import lax
from jax.experimental import pallas as pl
from jax.experimental.pallas import tpu as pltpu
from jax.sharding import PartitionSpec as P

norm_eps = 1e-06
rope_base = 1000000.0


def rms_scale(values, gain):
    return values * lax.rsqrt(jnp.mean(values * values, axis=-1, keepdims=True) + norm_eps) * gain


def angles(positions, size):
    half_size = size // 2
    freq = jnp.exp(jnp.arange(half_size, dtype=jnp.float32) * (-2.0 * math.log(rope_base) / size))
    turned = positions[:, None] * freq[None, :]
    return (jnp.cos(turned), jnp.sin(turned))


def rotate(values, cosine, sine):
    half_size = values.shape[-1] // 2
    first = values[..., :half_size]
    second = values[..., half_size:]
    return jnp.concatenate(
        [first * cosine - second * sine, second * cosine + first * sine], axis=-1
    )


def geglu(gate_pre, up_pre):
    return jax.nn.gelu(gate_pre, approximate=True) * up_pre


def contract_rows(left, right):
    return lax.dot_general(
        left, right, (((0,), (0,)), ((), ())), preferred_element_type=jnp.float32
    )


def contract_cols(left, right):
    return lax.dot_general(
        left, right, (((1,), (1,)), ((), ())), preferred_element_type=jnp.float32
    )


vmem_limit = 52 * 1024 * 1024


def greet(axes):
    barrier = pltpu.get_barrier_semaphore()
    count = 0
    for axis in axes:
        size = lax.axis_size(axis)
        me = lax.axis_index(axis)
        for step in range(1, size):
            pl.semaphore_signal(
                barrier,
                inc=1,
                device_id={axis: lax.rem(me + step, size)},
                device_id_type=pl.DeviceIdType.MESH,
            )
            count += 1
    pl.semaphore_wait(barrier, count)


def send(source, target, send_sem, recv_sem, axis, index):
    copy = pltpu.make_async_remote_copy(
        src_ref=source,
        dst_ref=target,
        send_sem=send_sem,
        recv_sem=recv_sem,
        device_id={axis: index},
        device_id_type=pl.DeviceIdType.MESH,
    )
    copy.start()
    return copy


def gather_kernel(first, second, x_ref, out_ref, own_sem, send_a, recv_a, send_b, recv_b):
    size_a, size_b = lax.axis_size(first), lax.axis_size(second)
    at_a, at_b = lax.axis_index(first), lax.axis_index(second)
    greet((first, second))
    own = out_ref.at[at_a, at_b]
    sent_a, sent_b = [], []
    for step in range(1, size_a):
        sent_a.append(
            send(x_ref, own, send_a.at[step - 1], recv_a.at[step - 1], first,
                 lax.rem(at_a + step, size_a))
        )
    for turn in range(1, size_b):
        sent_b.append(
            send(x_ref, own, send_b.at[turn - 1, 0], recv_b.at[turn - 1, 0], second,
                 lax.rem(at_b + turn, size_b))
        )
    keep = pltpu.make_async_copy(x_ref, own, own_sem)
    keep.start()
    for step in range(1, size_a):
        sent_a[step - 1].wait_recv()
        slot = out_ref.at[lax.rem(at_a + size_a - step, size_a), at_b]
        for turn in range(1, size_b):
            sent_b.append(
                send(slot, slot, send_b.at[turn - 1, step], recv_b.at[turn - 1, step], second,
                     lax.rem(at_b + turn, size_b))
            )
    for copy in sent_b:
        copy.wait_recv()
    for copy in sent_a + sent_b:
        copy.wait_send()
    keep.wait()


def gather(values, first, second, number):
    size_a, size_b = lax.axis_size(first), lax.axis_size(second)
    dma = pltpu.SemaphoreType.DMA
    return pl.pallas_call(
        functools.partial(gather_kernel, first, second),
        out_shape=jax.ShapeDtypeStruct((size_a, size_b) + values.shape, values.dtype),
        in_specs=[pl.BlockSpec(memory_space=pl.ANY)],
        out_specs=pl.BlockSpec(memory_space=pl.ANY),
        scratch_shapes=[
            dma,
            dma((size_a - 1,)),
            dma((size_a - 1,)),
            dma((size_b - 1, size_a)),
            dma((size_b - 1, size_a)),
        ],
        compiler_params=pltpu.CompilerParams(
            collective_id=number, has_side_effects=True, vmem_limit_bytes=vmem_limit
        ),
        name="gather_" + first + "_" + second,
    )(values)


def scatter_kernel(
    first, second, x_ref, out_ref, held_b, part, held_a, send_a, recv_a, send_b, recv_b
):
    size_a, size_b = lax.axis_size(first), lax.axis_size(second)
    at_a, at_b = lax.axis_index(first), lax.axis_index(second)
    greet((first, second))
    order = list(range(1, size_a)) + [0]
    sent_a, sent_b = {}, {}
    for step in order:
        goal = lax.rem(at_a + step, size_a)
        for turn in range(1, size_b):
            other = lax.rem(at_b + turn, size_b)
            sent_b[turn, step] = send(
                x_ref.at[goal, other], held_b.at[turn - 1, step],
                send_b.at[turn - 1, step], recv_b.at[turn - 1, step], second, other,
            )
    for step in order:
        goal = lax.rem(at_a + step, size_a)
        total = x_ref[goal, at_b].astype(jnp.float32)
        for turn in range(1, size_b):
            sent_b[turn, step].wait_recv()
            total += held_b[turn - 1, step].astype(jnp.float32)
        if step > 0:
            part[step - 1] = total.astype(part.dtype)
            sent_a[step] = send(
                part.at[step - 1], held_a.at[step - 1],
                send_a.at[step - 1], recv_a.at[step - 1], first, goal,
            )
        else:
            for back in range(1, size_a):
                sent_a[back].wait_recv()
                total += held_a[back - 1].astype(jnp.float32)
            out_ref[...] = total.astype(out_ref.dtype)
    for copy in list(sent_a.values()) + list(sent_b.values()):
        copy.wait_send()


def scatter_sum(values, first, second, number, dtype=jnp.float32):
    size_a, size_b = lax.axis_size(first), lax.axis_size(second)
    block = values.shape[2:]
    dma = pltpu.SemaphoreType.DMA
    return pl.pallas_call(
        functools.partial(scatter_kernel, first, second),
        out_shape=jax.ShapeDtypeStruct(block, dtype),
        in_specs=[pl.BlockSpec(memory_space=pltpu.VMEM)],
        out_specs=pl.BlockSpec(memory_space=pltpu.VMEM),
        scratch_shapes=[
            pltpu.VMEM((size_b - 1, size_a) + block, values.dtype),
            pltpu.VMEM((size_a - 1,) + block, values.dtype),
            pltpu.VMEM((size_a - 1,) + block, values.dtype),
            dma((size_a - 1,)),
            dma((size_a - 1,)),
            dma((size_b - 1, size_a)),
            dma((size_b - 1, size_a)),
        ],
        compiler_params=pltpu.CompilerParams(
            collective_id=number, has_side_effects=True, vmem_limit_bytes=vmem_limit
        ),
        name="scatter_" + first + "_" + second,
    )(values)


def greet_all(axes, head_steps):
    barrier = pltpu.get_barrier_semaphore()
    peers = []
    for axis in axes:
        size = lax.axis_size(axis)
        peers += [(axis, lax.rem(lax.axis_index(axis) + step, size)) for step in range(1, size)]
    peers += [("head", index) for index in head_steps]
    for axis, index in peers:
        pl.semaphore_signal(
            barrier, inc=1, device_id={axis: index}, device_id_type=pl.DeviceIdType.MESH
        )
    pl.semaphore_wait(barrier, len(peers))


def head_place():
    size = lax.axis_size("head")
    at_h = lax.axis_index("head")
    low_bit = lax.rem(at_h, 2)
    partner = at_h + 1 - 2 * low_bit
    likes = [lax.rem(at_h + 2 * step, size) for step in range(1, size // 2)]
    return at_h, low_bit, partner, likes


def weights_kernel(
    x_ref, out_ref, own_sem, send_a, recv_a, send_b, recv_b, send_h, recv_h, send_l, recv_l
):
    size_a, size_b, size_h = (lax.axis_size(axis) for axis in ("batch", "ctx", "head"))
    at_a, at_b = lax.axis_index("batch"), lax.axis_index("ctx")
    at_h, low_bit, partner, likes = head_place()
    greet_all(("batch", "ctx"), likes + [partner])
    own = out_ref.at[at_a, at_b, at_h]
    sent_a, sent_b, sent_h, sent_l = {}, {}, {}, {}
    for step in range(1, size_a):
        sent_a[step] = send(
            x_ref.at[at_h], own, send_a.at[step - 1], recv_a.at[step - 1], "batch",
            lax.rem(at_a + step, size_a),
        )

    def to_ctx(source, target, step):
        for turn in range(1, size_b):
            sent_b[step, turn] = send(
                source, target, send_b.at[step, turn - 1], recv_b.at[step, turn - 1], "ctx",
                lax.rem(at_b + turn, size_b),
            )

    to_ctx(x_ref.at[at_h], own, 0)
    keep = pltpu.make_async_copy(x_ref, out_ref.at[at_a, at_b], own_sem)
    keep.start()

    def slot(step, turn, head):
        return out_ref.at[
            lax.rem(at_a + size_a - step, size_a), lax.rem(at_b + size_b - turn, size_b), head
        ]

    def to_head(step, turn):
        here = slot(step, turn, at_h)
        for jump, like in enumerate(likes):
            sent_h[step, turn, jump] = send(
                here, here, send_h.at[step, turn, jump], recv_h.at[step, turn, jump], "head", like
            )
        sent_l[step, turn, 0] = send(
            here, here, send_l.at[step, turn, 0], recv_l.at[step, turn, 0], "head", partner
        )

    for step in range(1, size_a):
        sent_a[step].wait_recv()
        here = slot(step, 0, at_h)
        to_ctx(here, here, step)
        to_head(step, 0)
    for step in range(size_a):
        for turn in range(1, size_b):
            sent_b[step, turn].wait_recv()
            to_head(step, turn)
    for step, turn, jump in list(sent_h):
        sent_h[step, turn, jump].wait_recv()
        back = lax.rem(at_h + size_h - 2 * (jump + 1), size_h)
        here = slot(step, turn, back)
        sent_l[step, turn, jump + 1] = send(
            here, here, send_l.at[step, turn, jump + 1], recv_l.at[step, turn, jump + 1],
            "head", partner,
        )
    for copy in sent_l.values():
        copy.wait_recv()
    for sent in (sent_a, sent_b, sent_h, sent_l):
        for copy in sent.values():
            copy.wait_send()
    keep.wait()


def gather_weights(values, number):
    size_a, size_b, size_h = (lax.axis_size(axis) for axis in ("batch", "ctx", "head"))
    dma = pltpu.SemaphoreType.DMA
    pairs = size_h // 2
    return pl.pallas_call(
        weights_kernel,
        out_shape=jax.ShapeDtypeStruct((size_a, size_b) + values.shape, values.dtype),
        in_specs=[pl.BlockSpec(memory_space=pl.ANY)],
        out_specs=pl.BlockSpec(memory_space=pl.ANY),
        scratch_shapes=[dma]
        + [dma((size_a - 1,))] * 2
        + [dma((size_a, size_b - 1))] * 2
        + [dma((size_a, size_b, pairs - 1))] * 2
        + [dma((size_a, size_b, pairs))] * 2,
        compiler_params=pltpu.CompilerParams(
            collective_id=number, has_side_effects=True, vmem_limit_bytes=vmem_limit
        ),
        name="gather_weights",
    )(values)


def grads_kernel(
    x_ref, w_ref, out_ref, wout_ref,
    r_low, p_ctx, r_ctx, p_batch, r_batch, p_like, r_like, w_low, wp_like, w_like,
    send_low, recv_low, send_c, recv_c, send_b, recv_b, send_k, recv_k, send_o, recv_o,
    wsend_low, wrecv_low, wsend_k, wrecv_k, wsend_h, wrecv_h, wsend_o, wrecv_o,
):
    f32 = jnp.float32
    size_a, size_b, size_h = (lax.axis_size(axis) for axis in ("batch", "ctx", "head"))
    at_a, at_b = lax.axis_index("batch"), lax.axis_index("ctx")
    at_h, low_bit, partner, likes = head_place()
    pairs = size_h // 2
    other = 1 - low_bit
    greet_all(("batch", "ctx"), likes + [partner])
    order = list(range(1, size_a)) + [0]
    turns = list(range(1, size_b)) + [0]

    def goal(step, turn):
        return lax.rem(at_a + step, size_a), lax.rem(at_b + turn, size_b)

    low_sent, ctx_sent, batch_sent, like_sent = {}, {}, {}, {}
    w_low_sent, w_like_sent, w_all, w_out = {}, {}, {}, {}
    for turn in turns:
        for step in order:
            goal_a, goal_b = goal(step, turn)
            low_sent[step, turn] = send(
                x_ref.at[goal_a, goal_b, other], r_low.at[step, turn],
                send_low.at[step, turn], recv_low.at[step, turn], "head", partner,
            )
    for jump in list(range(1, pairs)) + [0]:
        theirs = lax.rem(partner + 2 * jump, size_h)
        w_low_sent[jump] = send(
            w_ref.at[theirs], w_low.at[jump], wsend_low.at[jump], wrecv_low.at[jump],
            "head", partner,
        )

    def pair_sum(step, turn):
        goal_a, goal_b = goal(step, turn)
        low_sent[step, turn].wait_recv()
        return x_ref[goal_a, goal_b, low_bit].astype(f32) + r_low[step, turn].astype(f32)

    for turn in range(1, size_b):
        for step in order:
            p_ctx[step, turn - 1] = pair_sum(step, turn).astype(p_ctx.dtype)
            ctx_sent[step, turn] = send(
                p_ctx.at[step, turn - 1], r_ctx.at[step, turn - 1],
                send_c.at[step, turn - 1], recv_c.at[step, turn - 1], "ctx", goal(step, turn)[1],
            )
    for jump in range(1, pairs):
        w_low_sent[jump].wait_recv()
        like = likes[jump - 1]
        wp_like[jump - 1] = (w_ref[like].astype(f32) + w_low[jump].astype(f32)).astype(
            wp_like.dtype
        )
        w_like_sent[jump] = send(
            wp_like.at[jump - 1], w_like.at[jump - 1],
            wsend_k.at[jump - 1], wrecv_k.at[jump - 1], "head", like,
        )

    def ctx_sum(step):
        total = pair_sum(step, 0)
        for turn in range(1, size_b):
            ctx_sent[step, turn].wait_recv()
            total += r_ctx[step, turn - 1].astype(f32)
        return total

    for step in range(1, size_a):
        p_batch[step - 1] = ctx_sum(step).astype(p_batch.dtype)
        batch_sent[step] = send(
            p_batch.at[step - 1], r_batch.at[step - 1],
            send_b.at[step - 1], recv_b.at[step - 1], "batch", goal(step, 0)[0],
        )
    total = ctx_sum(0)
    w_low_sent[0].wait_recv()
    w_total = w_ref[at_h].astype(f32) + w_low[0].astype(f32)
    for jump in range(1, pairs):
        w_like_sent[jump].wait_recv()
        w_total += w_like[jump - 1].astype(f32)
    wout_ref[at_h] = w_total.astype(wout_ref.dtype)
    w_own = wout_ref.at[at_h]
    for jump in range(1, pairs):
        w_all[jump] = send(
            w_own, w_own, wsend_h.at[jump - 1], wrecv_h.at[jump - 1], "head", likes[jump - 1]
        )
    w_out[0] = send(w_own, w_own, wsend_o.at[0], wrecv_o.at[0], "head", partner)

    for step in range(1, size_a):
        batch_sent[step].wait_recv()
        total += r_batch[step - 1].astype(f32)
    p_like[...] = total.astype(p_like.dtype)
    for jump in range(1, pairs):
        like_sent[jump] = send(
            p_like, r_like.at[jump - 1], send_k.at[jump - 1], recv_k.at[jump - 1],
            "head", likes[jump - 1],
        )
    for jump in range(1, pairs):
        w_all[jump].wait_recv()
        slot = wout_ref.at[lax.rem(at_h + size_h - 2 * jump, size_h)]
        w_out[jump] = send(slot, slot, wsend_o.at[jump], wrecv_o.at[jump], "head", partner)
    total = p_like[...].astype(f32)
    for jump in range(1, pairs):
        like_sent[jump].wait_recv()
        total += r_like[jump - 1].astype(f32)
    out_ref[low_bit] = total.astype(out_ref.dtype)
    last = send(out_ref.at[low_bit], out_ref.at[low_bit], send_o, recv_o, "head", partner)
    for copy in w_out.values():
        copy.wait_recv()
    last.wait_recv()
    last.wait_send()
    for sent in (
        low_sent, ctx_sent, batch_sent, like_sent, w_low_sent, w_like_sent, w_all, w_out
    ):
        for copy in sent.values():
            copy.wait_send()


def sum_grads(values, wide, number):
    size_a, size_b, size_h = (lax.axis_size(axis) for axis in ("batch", "ctx", "head"))
    pairs = size_h // 2
    block, wide_block = values.shape[3:], wide.shape[1:]
    kind = values.dtype
    dma = pltpu.SemaphoreType.DMA
    vmem = pl.BlockSpec(memory_space=pltpu.VMEM)
    return pl.pallas_call(
        grads_kernel,
        out_shape=(
            jax.ShapeDtypeStruct((2,) + block, kind),
            jax.ShapeDtypeStruct(wide.shape, kind),
        ),
        in_specs=[vmem, vmem],
        out_specs=(vmem, vmem),
        scratch_shapes=[
            pltpu.VMEM((size_a, size_b) + block, kind),
            pltpu.VMEM((size_a, size_b - 1) + block, kind),
            pltpu.VMEM((size_a, size_b - 1) + block, kind),
            pltpu.VMEM((size_a - 1,) + block, kind),
            pltpu.VMEM((size_a - 1,) + block, kind),
            pltpu.VMEM(block, kind),
            pltpu.VMEM((pairs - 1,) + block, kind),
            pltpu.VMEM((pairs,) + wide_block, kind),
            pltpu.VMEM((pairs - 1,) + wide_block, kind),
            pltpu.VMEM((pairs - 1,) + wide_block, kind),
        ]
        + [dma((size_a, size_b))] * 2
        + [dma((size_a, size_b - 1))] * 2
        + [dma((size_a - 1,))] * 2
        + [dma((pairs - 1,))] * 2
        + [dma] * 2
        + [dma((pairs,))] * 2
        + [dma((pairs - 1,))] * 4
        + [dma((pairs,))] * 2,
        compiler_params=pltpu.CompilerParams(
            collective_id=number, has_side_effects=True, vmem_limit_bytes=vmem_limit
        ),
        name="sum_grads",
    )(values, wide)


def local(
    tokens,
    attn_in_gain,
    query_weight,
    key_weight,
    value_weight,
    query_gain,
    key_gain,
    out_weight,
    attn_out_gain,
    ffn_in_gain,
    gate_weight,
    up_weight,
    down_weight,
    ffn_out_gain,
    cotangent,
):
    low = jnp.bfloat16
    size_b, size_c, size_h = (lax.axis_size(axis) for axis in ("batch", "ctx", "head"))
    ctx_index = lax.axis_index("ctx")
    head_index = lax.axis_index("head")
    tok, width = tokens.shape[1:]
    head_dim = key_gain.shape[0]
    n_q, n_k, n_o = query_weight.shape[1], key_weight.shape[1], out_weight.shape[0]
    shards = size_b * size_c
    heads = n_q * shards // head_dim
    scale = head_dim ** (-0.5)

    packed = jnp.concatenate([query_weight.T, key_weight.T, value_weight.T, out_weight], axis=0)
    packed = jnp.pad(packed, ((0, -packed.shape[0] % (16 * size_h)), (0, 0)))
    full = gather_weights(packed.reshape(size_h, -1, width), 0).reshape(shards, -1, width)
    full_q = full[:, :n_q].reshape(-1, width)
    full_k = full[:, n_q : n_q + n_k].reshape(-1, width)
    full_v = full[:, n_q + n_k : n_q + 2 * n_k].reshape(-1, width)
    full_o = full[:, n_q + 2 * n_k : n_q + 2 * n_k + n_o].reshape(-1, width)

    inputs = tokens[0].astype(jnp.float32)
    first_pos = (ctx_index * size_h + head_index) * tok
    query_pos = first_pos + jnp.arange(tok, dtype=jnp.int32)
    cosine, sine = angles(query_pos.astype(jnp.float32), head_dim)
    normed_f, pull_in = jax.vjp(rms_scale, inputs, attn_in_gain)
    normed_in = normed_f.astype(low)
    query_raw = contract_cols(normed_in, full_q).reshape(tok, heads, head_dim)
    key_raw = contract_cols(normed_in, full_k)
    value_low = contract_cols(normed_in, full_v).astype(low)

    def query_path(values, gain):
        return rotate(rms_scale(values, gain), cosine[:, None, :], sine[:, None, :])

    def key_path(values, gain):
        return rotate(rms_scale(values, gain), cosine, sine)

    query_rot, pull_query = jax.vjp(query_path, query_raw, query_gain)
    key_rot, pull_key = jax.vjp(key_path, key_raw, key_gain)
    key_low = key_rot.astype(low)
    rows = heads * tok
    query_rows = query_rot.astype(low).transpose(1, 0, 2).reshape(rows, head_dim)
    pairs = gather(jnp.concatenate([key_low, value_low], axis=1), "ctx", "head", 1)
    pairs = pairs.reshape(-1, 2 * head_dim)
    key_rows, value_rows = pairs[:, :head_dim], pairs[:, head_dim:]
    length = key_rows.shape[0]

    scores = contract_cols(query_rows, key_rows) * scale
    key_pos = jnp.arange(length, dtype=jnp.int32)
    row_pos = jnp.tile(query_pos, heads)
    scores = jnp.where(key_pos[None, :] <= row_pos[:, None], scores, -jnp.inf)
    row_max = jnp.max(scores, axis=1, keepdims=True)
    raised = jnp.exp(scores - row_max)
    probs = raised * (1.0 / jnp.sum(raised, axis=1, keepdims=True))
    probs_low = probs.astype(low)
    attended = jnp.dot(probs_low, value_rows, preferred_element_type=jnp.float32)

    def to_tokens(values):
        return values.reshape(heads, tok, head_dim).transpose(1, 0, 2).reshape(tok, -1)

    attended_tok = to_tokens(attended.astype(low))
    projected = jnp.dot(attended_tok, full_o, preferred_element_type=jnp.float32)
    post_attn, pull_aout = jax.vjp(rms_scale, projected, attn_out_gain)
    resid = inputs + post_attn
    normed_ffn_f, pull_fin = jax.vjp(rms_scale, resid, ffn_in_gain)
    group_ffn = gather(normed_ffn_f.astype(low), "batch", "ctx", 2).reshape(-1, width)
    gate_pre = jnp.dot(group_ffn, gate_weight, preferred_element_type=jnp.float32)
    up_pre = jnp.dot(group_ffn, up_weight, preferred_element_type=jnp.float32)
    hidden_f, pull_glu = jax.vjp(geglu, gate_pre, up_pre)
    hidden = hidden_f.astype(low)
    mixed_part = jnp.dot(hidden, down_weight, preferred_element_type=jnp.float32).astype(low)
    mixed = scatter_sum(mixed_part.reshape(size_b, size_c, tok, width), "batch", "ctx", 3)
    post_ffn, pull_fout = jax.vjp(rms_scale, mixed, ffn_out_gain)
    block_out = (resid + post_ffn).astype(low)

    out_grad = cotangent[0].astype(jnp.float32)
    mixed_grad_f, fout_gain_grad = pull_fout(out_grad)
    mixed_grad = gather(mixed_grad_f.astype(low), "batch", "ctx", 4).reshape(-1, width)
    hidden_grad = contract_cols(mixed_grad, down_weight)
    gate_grad_f, up_grad_f = pull_glu(hidden_grad)
    gate_grad = gate_grad_f.astype(low)
    up_grad = up_grad_f.astype(low)
    ffn_part = (contract_cols(gate_grad, gate_weight) + contract_cols(up_grad, up_weight)).astype(
        low
    )
    normed_ffn_grad = scatter_sum(ffn_part.reshape(size_b, size_c, tok, width), "batch", "ctx", 5)
    down_grad = contract_rows(hidden, mixed_grad).astype(low)
    gate_w_grad = contract_rows(gate_grad, group_ffn).astype(low)
    up_w_grad = contract_rows(up_grad, group_ffn).astype(low)
    resid_part, fin_gain_grad = pull_fin(normed_ffn_grad)
    resid_grad = out_grad + resid_part
    projected_grad_f, aout_gain_grad = pull_aout(resid_grad)
    projected_grad = projected_grad_f.astype(low)
    out_w_grad = contract_rows(attended_tok, projected_grad).astype(low)
    attended_grad = contract_cols(projected_grad, full_o).astype(low)
    grad_rows = attended_grad.reshape(tok, heads, head_dim).transpose(1, 0, 2).reshape(rows, head_dim)
    delta = jnp.sum(grad_rows.astype(jnp.float32) * attended, axis=1)

    probs_grad = contract_cols(grad_rows, value_rows)
    score_grad = (probs * (probs_grad - delta[:, None])).astype(low)
    query_low_grad = jnp.dot(score_grad, key_rows, preferred_element_type=jnp.float32) * scale
    key_part = contract_rows(score_grad, query_rows) * scale
    value_part = contract_rows(probs_low, grad_rows)
    pair_part = jnp.concatenate([key_part.astype(low), value_part.astype(low)], axis=1)
    pair_grad = scatter_sum(
        pair_part.reshape(size_c, size_h, tok, 2 * head_dim), "ctx", "head", 6
    )
    key_low_grad, value_grad = pair_grad[:, :head_dim], pair_grad[:, head_dim:].astype(low)
    query_low_grad = to_tokens(query_low_grad.astype(low)).reshape(tok, heads, head_dim)
    query_raw_grad_f, query_gain_grad = pull_query(query_low_grad.astype(jnp.float32))
    key_raw_grad_f, key_gain_grad = pull_key(key_low_grad)
    query_raw_grad = query_raw_grad_f.reshape(tok, heads * head_dim).astype(low)
    key_raw_grad = key_raw_grad_f.astype(low)
    query_w_grad = contract_rows(query_raw_grad, normed_in).astype(low)
    key_w_grad = contract_rows(key_raw_grad, normed_in).astype(low)
    value_w_grad = contract_rows(value_grad, normed_in).astype(low)
    normed_in_grad = (
        jnp.dot(query_raw_grad, full_q, preferred_element_type=jnp.float32)
        + jnp.dot(key_raw_grad, full_k, preferred_element_type=jnp.float32)
        + jnp.dot(value_grad, full_v, preferred_element_type=jnp.float32)
    )
    inputs_part, ain_gain_grad = pull_in(normed_in_grad)
    inputs_grad = resid_grad + inputs_part

    gains = (
        ain_gain_grad,
        query_gain_grad,
        key_gain_grad,
        aout_gain_grad,
        fin_gain_grad,
        fout_gain_grad,
    )
    gain_flat = jnp.concatenate(gains)
    gain_rows = -(-gain_flat.shape[0] // width)
    fixed = n_q + 2 * n_k + n_o
    gain_pad = gain_rows + -(fixed + gain_rows) % 32
    gain_block = jnp.pad(gain_flat, (0, gain_pad * width - gain_flat.shape[0])).astype(low)
    gain_block = jnp.broadcast_to(gain_block.reshape(1, gain_pad, width), (shards, gain_pad, width))
    split = (
        query_w_grad.reshape(shards, n_q, width),
        key_w_grad.reshape(shards, n_k, width),
        value_w_grad.reshape(shards, n_k, width),
        out_w_grad.reshape(shards, n_o, width),
        gain_block,
    )
    grads = jnp.concatenate(split, axis=1)
    wide = jnp.concatenate([gate_w_grad, up_w_grad, down_grad], axis=0)
    wide = jnp.pad(wide, ((0, -wide.shape[0] % (16 * size_h)), (0, 0)))
    done, wide_done = sum_grads(
        grads.reshape(size_b, size_c, 2, -1, width), wide.reshape(size_h, -1, width), 7
    )
    done = jnp.concatenate(
        [done.reshape(-1, width), wide_done.reshape(-1, width)], axis=0
    ).astype(jnp.float32)

    parts = []
    start = 0
    n_f = gate_weight.shape[1]
    for count in (n_q, n_k, n_k, n_o, gain_pad, n_f, n_f, n_f):
        parts.append(done[start : start + count])
        start += count
    gain_done = parts[4].reshape(-1)
    gain_out = []
    start = 0
    for gain in gains:
        gain_out.append(gain_done[start : start + gain.shape[0]])
        start += gain.shape[0]
    return (
        block_out[None],
        inputs_grad[None],
        gain_out[0],
        parts[0].T,
        parts[1].T,
        parts[2].T,
        gain_out[1],
        gain_out[2],
        parts[3],
        gain_out[3],
        gain_out[4],
        parts[5].T,
        parts[6].T,
        parts[7],
        gain_out[5],
    )


def solution(mesh):
    in_specs = (
        P("batch", ("ctx", "head"), None),
        P(),
        P(None, ("batch", "ctx")),
        P(None, ("batch", "ctx")),
        P(None, ("batch", "ctx")),
        P(),
        P(),
        P(("batch", "ctx"), None),
        P(),
        P(),
        P(None, ("batch", "ctx")),
        P(None, ("batch", "ctx")),
        P(("batch", "ctx"), None),
        P(),
        P("batch", ("ctx", "head"), None),
    )
    out_specs = (
        P("batch", ("ctx", "head"), None),
        P("batch", ("ctx", "head"), None),
        P(),
        P(None, ("batch", "ctx")),
        P(None, ("batch", "ctx")),
        P(None, ("batch", "ctx")),
        P(),
        P(),
        P(("batch", "ctx"), None),
        P(),
        P(),
        P(None, ("batch", "ctx")),
        P(None, ("batch", "ctx")),
        P(("batch", "ctx"), None),
        P(),
    )
    return jax.shard_map(local, mesh=mesh, in_specs=in_specs, out_specs=out_specs, check_vma=False)
```

```python
import functools
import math

import jax
import jax.numpy as jnp
from jax import lax
from jax.experimental import pallas as pl
from jax.experimental.pallas import tpu as pltpu
from jax.sharding import PartitionSpec as P

norm_eps = 1e-06
rope_base = 1000000.0


def rms_scale(values, gain):
    return values * lax.rsqrt(jnp.mean(values * values, axis=-1, keepdims=True) + norm_eps) * gain


def angles(positions, size):
    half_size = size // 2
    freq = jnp.exp(jnp.arange(half_size, dtype=jnp.float32) * (-2.0 * math.log(rope_base) / size))
    turned = positions[:, None] * freq[None, :]
    return (jnp.cos(turned), jnp.sin(turned))


def rotate(values, cosine, sine):
    half_size = values.shape[-1] // 2
    first = values[..., :half_size]
    second = values[..., half_size:]
    return jnp.concatenate(
        [first * cosine - second * sine, second * cosine + first * sine], axis=-1
    )


def geglu(gate_pre, up_pre):
    return jax.nn.gelu(gate_pre, approximate=True) * up_pre


def contract_rows(left, right):
    return lax.dot_general(
        left, right, (((0,), (0,)), ((), ())), preferred_element_type=jnp.float32
    )


def contract_cols(left, right):
    return lax.dot_general(
        left, right, (((1,), (1,)), ((), ())), preferred_element_type=jnp.float32
    )


vmem_limit = 52 * 1024 * 1024


def greet(axes):
    barrier = pltpu.get_barrier_semaphore()
    count = 0
    for axis in axes:
        size = lax.axis_size(axis)
        me = lax.axis_index(axis)
        for step in range(1, size):
            pl.semaphore_signal(
                barrier,
                inc=1,
                device_id={axis: lax.rem(me + step, size)},
                device_id_type=pl.DeviceIdType.MESH,
            )
            count += 1
    pl.semaphore_wait(barrier, count)


def send(source, target, send_sem, recv_sem, axis, index):
    copy = pltpu.make_async_remote_copy(
        src_ref=source,
        dst_ref=target,
        send_sem=send_sem,
        recv_sem=recv_sem,
        device_id={axis: index},
        device_id_type=pl.DeviceIdType.MESH,
    )
    copy.start()
    return copy


def gather_kernel(first, second, x_ref, out_ref, own_sem, send_a, recv_a, send_b, recv_b):
    size_a, size_b = lax.axis_size(first), lax.axis_size(second)
    at_a, at_b = lax.axis_index(first), lax.axis_index(second)
    greet((first, second))
    own = out_ref.at[at_a, at_b]

    def along(source, target, way, step, goal):
        return pltpu.make_async_remote_copy(
            src_ref=source,
            dst_ref=target,
            send_sem=send_a.at[way, step],
            recv_sem=recv_a.at[way, step],
            device_id={first: goal},
            device_id_type=pl.DeviceIdType.MESH,
        )

    def across(source, target, way, step):
        return [
            pltpu.make_async_remote_copy(
                src_ref=source,
                dst_ref=target,
                send_sem=send_b.at[turn - 1, way, step],
                recv_sem=recv_b.at[turn - 1, way, step],
                device_id={second: lax.rem(at_b + turn, size_b)},
                device_id_type=pl.DeviceIdType.MESH,
            )
            for turn in range(1, size_b)
        ]

    ups = at_a < size_a - 1
    downs = at_a > 0
    ahead = lax.rem(at_a + 1, size_a)
    behind = lax.rem(at_a + size_a - 1, size_a)
    pl.when(ups)(lambda: along(x_ref, own, 0, 0, ahead).start())
    pl.when(downs)(lambda: along(x_ref, own, 1, 0, behind).start())
    for copy in across(x_ref, own, 0, 0):
        copy.start()
    keep = pltpu.make_async_copy(x_ref, own, own_sem)
    keep.start()

    def hand_on(way, step):
        source = at_a - step if way == 0 else at_a + step
        slot = out_ref.at[source, at_b]
        goal = ahead if way == 0 else behind
        along(slot, slot, way, step - 1, goal).wait_recv()
        pl.when(ups if way == 0 else downs)(lambda: along(slot, slot, way, step, goal).start())
        for copy in across(slot, slot, way, step):
            copy.start()

    def finish(way, step):
        source = at_a - step if way == 0 else at_a + step
        slot = out_ref.at[source, at_b]
        goal = ahead if way == 0 else behind
        for copy in across(slot, slot, way, step):
            copy.wait()
        pl.when(ups if way == 0 else downs)(lambda: along(slot, slot, way, step, goal).wait_send())

    for stage in (hand_on, finish):
        for step in range(1, size_a):
            pl.when(at_a >= step)(functools.partial(stage, 0, step))
            pl.when(at_a < size_a - step)(functools.partial(stage, 1, step))
    for copy in across(x_ref, own, 0, 0):
        copy.wait()
    pl.when(ups)(lambda: along(x_ref, own, 0, 0, ahead).wait_send())
    pl.when(downs)(lambda: along(x_ref, own, 1, 0, behind).wait_send())
    keep.wait()


def gather(values, first, second, number):
    size_a, size_b = lax.axis_size(first), lax.axis_size(second)
    dma = pltpu.SemaphoreType.DMA
    return pl.pallas_call(
        functools.partial(gather_kernel, first, second),
        out_shape=jax.ShapeDtypeStruct((size_a, size_b) + values.shape, values.dtype),
        in_specs=[pl.BlockSpec(memory_space=pl.ANY)],
        out_specs=pl.BlockSpec(memory_space=pl.ANY),
        scratch_shapes=[dma]
        + [dma((2, size_a))] * 2
        + [dma((size_b - 1, 2, size_a))] * 2,
        compiler_params=pltpu.CompilerParams(
            collective_id=number, has_side_effects=True, vmem_limit_bytes=vmem_limit
        ),
        name="gather_" + first + "_" + second,
    )(values)


def scatter_kernel(
    first, second, x_ref, out_ref, held_b, part, held_a, send_a, recv_a, send_b, recv_b
):
    size_a, size_b = lax.axis_size(first), lax.axis_size(second)
    at_a, at_b = lax.axis_index(first), lax.axis_index(second)
    greet((first, second))
    order = list(range(1, size_a)) + [0]
    sent_a, sent_b = {}, {}
    for step in order:
        goal = lax.rem(at_a + step, size_a)
        for turn in range(1, size_b):
            other = lax.rem(at_b + turn, size_b)
            sent_b[turn, step] = send(
                x_ref.at[goal, other], held_b.at[turn - 1, step],
                send_b.at[turn - 1, step], recv_b.at[turn - 1, step], second, other,
            )
    for step in order:
        goal = lax.rem(at_a + step, size_a)
        total = x_ref[goal, at_b].astype(jnp.float32)
        for turn in range(1, size_b):
            sent_b[turn, step].wait_recv()
            total += held_b[turn - 1, step].astype(jnp.float32)
        if step > 0:
            part[step - 1] = total.astype(part.dtype)
            sent_a[step] = send(
                part.at[step - 1], held_a.at[step - 1],
                send_a.at[step - 1], recv_a.at[step - 1], first, goal,
            )
        else:
            for back in range(1, size_a):
                sent_a[back].wait_recv()
                total += held_a[back - 1].astype(jnp.float32)
            out_ref[...] = total.astype(out_ref.dtype)
    for copy in list(sent_a.values()) + list(sent_b.values()):
        copy.wait_send()


def scatter_sum(values, first, second, number, dtype=jnp.float32):
    size_a, size_b = lax.axis_size(first), lax.axis_size(second)
    block = values.shape[2:]
    dma = pltpu.SemaphoreType.DMA
    return pl.pallas_call(
        functools.partial(scatter_kernel, first, second),
        out_shape=jax.ShapeDtypeStruct(block, dtype),
        in_specs=[pl.BlockSpec(memory_space=pltpu.VMEM)],
        out_specs=pl.BlockSpec(memory_space=pltpu.VMEM),
        scratch_shapes=[
            pltpu.VMEM((size_b - 1, size_a) + block, values.dtype),
            pltpu.VMEM((size_a - 1,) + block, values.dtype),
            pltpu.VMEM((size_a - 1,) + block, values.dtype),
            dma((size_a - 1,)),
            dma((size_a - 1,)),
            dma((size_b - 1, size_a)),
            dma((size_b - 1, size_a)),
        ],
        compiler_params=pltpu.CompilerParams(
            collective_id=number, has_side_effects=True, vmem_limit_bytes=vmem_limit
        ),
        name="scatter_" + first + "_" + second,
    )(values)


def greet_all(axes, head_steps):
    barrier = pltpu.get_barrier_semaphore()
    peers = []
    for axis in axes:
        size = lax.axis_size(axis)
        peers += [(axis, lax.rem(lax.axis_index(axis) + step, size)) for step in range(1, size)]
    peers += [("head", index) for index in head_steps]
    for axis, index in peers:
        pl.semaphore_signal(
            barrier, inc=1, device_id={axis: index}, device_id_type=pl.DeviceIdType.MESH
        )
    pl.semaphore_wait(barrier, len(peers))


def head_place():
    size = lax.axis_size("head")
    at_h = lax.axis_index("head")
    low_bit = lax.rem(at_h, 2)
    partner = at_h + 1 - 2 * low_bit
    likes = [lax.rem(at_h + 2 * step, size) for step in range(1, size // 2)]
    return at_h, low_bit, partner, likes


def weights_kernel(
    x_ref, out_ref, own_sem, send_a, recv_a, send_b, recv_b, send_h, recv_h, send_l, recv_l
):
    size_a, size_b, size_h = (lax.axis_size(axis) for axis in ("batch", "ctx", "head"))
    at_a, at_b = lax.axis_index("batch"), lax.axis_index("ctx")
    at_h, low_bit, partner, likes = head_place()
    greet_all(("batch", "ctx"), likes + [partner])
    own = out_ref.at[at_a, at_b, at_h]
    sent_a, sent_b, sent_h, sent_l = {}, {}, {}, {}
    for step in range(1, size_a):
        sent_a[step] = send(
            x_ref.at[at_h], own, send_a.at[step - 1], recv_a.at[step - 1], "batch",
            lax.rem(at_a + step, size_a),
        )

    def to_ctx(source, target, step):
        for turn in range(1, size_b):
            sent_b[step, turn] = send(
                source, target, send_b.at[step, turn - 1], recv_b.at[step, turn - 1], "ctx",
                lax.rem(at_b + turn, size_b),
            )

    to_ctx(x_ref.at[at_h], own, 0)
    keep = pltpu.make_async_copy(x_ref, out_ref.at[at_a, at_b], own_sem)
    keep.start()

    def slot(step, turn, head):
        return out_ref.at[
            lax.rem(at_a + size_a - step, size_a), lax.rem(at_b + size_b - turn, size_b), head
        ]

    def to_head(step, turn):
        here = slot(step, turn, at_h)
        for jump, like in enumerate(likes):
            sent_h[step, turn, jump] = send(
                here, here, send_h.at[step, turn, jump], recv_h.at[step, turn, jump], "head", like
            )
        sent_l[step, turn, 0] = send(
            here, here, send_l.at[step, turn, 0], recv_l.at[step, turn, 0], "head", partner
        )

    for step in range(1, size_a):
        sent_a[step].wait_recv()
        here = slot(step, 0, at_h)
        to_ctx(here, here, step)
        to_head(step, 0)
    for step in range(size_a):
        for turn in range(1, size_b):
            sent_b[step, turn].wait_recv()
            to_head(step, turn)
    for step, turn, jump in list(sent_h):
        sent_h[step, turn, jump].wait_recv()
        back = lax.rem(at_h + size_h - 2 * (jump + 1), size_h)
        here = slot(step, turn, back)
        sent_l[step, turn, jump + 1] = send(
            here, here, send_l.at[step, turn, jump + 1], recv_l.at[step, turn, jump + 1],
            "head", partner,
        )
    for copy in sent_l.values():
        copy.wait_recv()
    for sent in (sent_a, sent_b, sent_h, sent_l):
        for copy in sent.values():
            copy.wait_send()
    keep.wait()


def gather_weights(values, number):
    size_a, size_b, size_h = (lax.axis_size(axis) for axis in ("batch", "ctx", "head"))
    dma = pltpu.SemaphoreType.DMA
    pairs = size_h // 2
    return pl.pallas_call(
        weights_kernel,
        out_shape=jax.ShapeDtypeStruct((size_a, size_b) + values.shape, values.dtype),
        in_specs=[pl.BlockSpec(memory_space=pl.ANY)],
        out_specs=pl.BlockSpec(memory_space=pl.ANY),
        scratch_shapes=[dma]
        + [dma((size_a - 1,))] * 2
        + [dma((size_a, size_b - 1))] * 2
        + [dma((size_a, size_b, pairs - 1))] * 2
        + [dma((size_a, size_b, pairs))] * 2,
        compiler_params=pltpu.CompilerParams(
            collective_id=number, has_side_effects=True, vmem_limit_bytes=vmem_limit
        ),
        name="gather_weights",
    )(values)


def grads_kernel(
    x_ref, w_ref, out_ref, wout_ref,
    r_low, p_ctx, r_ctx, p_batch, r_batch, p_like, r_like, w_low, wp_like, w_like,
    send_low, recv_low, send_c, recv_c, send_b, recv_b, send_k, recv_k, send_o, recv_o,
    wsend_low, wrecv_low, wsend_k, wrecv_k, wsend_h, wrecv_h, wsend_o, wrecv_o,
):
    f32 = jnp.float32
    size_a, size_b, size_h = (lax.axis_size(axis) for axis in ("batch", "ctx", "head"))
    at_a, at_b = lax.axis_index("batch"), lax.axis_index("ctx")
    at_h, low_bit, partner, likes = head_place()
    pairs = size_h // 2
    other = 1 - low_bit
    greet_all(("batch", "ctx"), likes + [partner])
    order = list(range(1, size_a)) + [0]
    turns = list(range(1, size_b)) + [0]

    def goal(step, turn):
        return lax.rem(at_a + step, size_a), lax.rem(at_b + turn, size_b)

    low_sent, ctx_sent, batch_sent, like_sent = {}, {}, {}, {}
    w_low_sent, w_like_sent, w_all, w_out = {}, {}, {}, {}
    for turn in turns:
        for step in order:
            goal_a, goal_b = goal(step, turn)
            low_sent[step, turn] = send(
                x_ref.at[goal_a, goal_b, other], r_low.at[step, turn],
                send_low.at[step, turn], recv_low.at[step, turn], "head", partner,
            )
    for jump in list(range(1, pairs)) + [0]:
        theirs = lax.rem(partner + 2 * jump, size_h)
        w_low_sent[jump] = send(
            w_ref.at[theirs], w_low.at[jump], wsend_low.at[jump], wrecv_low.at[jump],
            "head", partner,
        )

    def pair_sum(step, turn):
        goal_a, goal_b = goal(step, turn)
        low_sent[step, turn].wait_recv()
        return x_ref[goal_a, goal_b, low_bit].astype(f32) + r_low[step, turn].astype(f32)

    for turn in range(1, size_b):
        for step in order:
            p_ctx[step, turn - 1] = pair_sum(step, turn).astype(p_ctx.dtype)
            ctx_sent[step, turn] = send(
                p_ctx.at[step, turn - 1], r_ctx.at[step, turn - 1],
                send_c.at[step, turn - 1], recv_c.at[step, turn - 1], "ctx", goal(step, turn)[1],
            )
    for jump in range(1, pairs):
        w_low_sent[jump].wait_recv()
        like = likes[jump - 1]
        wp_like[jump - 1] = (w_ref[like].astype(f32) + w_low[jump].astype(f32)).astype(
            wp_like.dtype
        )
        w_like_sent[jump] = send(
            wp_like.at[jump - 1], w_like.at[jump - 1],
            wsend_k.at[jump - 1], wrecv_k.at[jump - 1], "head", like,
        )

    def ctx_sum(step):
        total = pair_sum(step, 0)
        for turn in range(1, size_b):
            ctx_sent[step, turn].wait_recv()
            total += r_ctx[step, turn - 1].astype(f32)
        return total

    for step in range(1, size_a):
        p_batch[step - 1] = ctx_sum(step).astype(p_batch.dtype)
        batch_sent[step] = send(
            p_batch.at[step - 1], r_batch.at[step - 1],
            send_b.at[step - 1], recv_b.at[step - 1], "batch", goal(step, 0)[0],
        )
    total = ctx_sum(0)
    w_low_sent[0].wait_recv()
    w_total = w_ref[at_h].astype(f32) + w_low[0].astype(f32)
    for jump in range(1, pairs):
        w_like_sent[jump].wait_recv()
        w_total += w_like[jump - 1].astype(f32)
    wout_ref[at_h] = w_total.astype(wout_ref.dtype)
    w_own = wout_ref.at[at_h]
    for jump in range(1, pairs):
        w_all[jump] = send(
            w_own, w_own, wsend_h.at[jump - 1], wrecv_h.at[jump - 1], "head", likes[jump - 1]
        )
    w_out[0] = send(w_own, w_own, wsend_o.at[0], wrecv_o.at[0], "head", partner)

    for step in range(1, size_a):
        batch_sent[step].wait_recv()
        total += r_batch[step - 1].astype(f32)
    p_like[...] = total.astype(p_like.dtype)
    for jump in range(1, pairs):
        like_sent[jump] = send(
            p_like, r_like.at[jump - 1], send_k.at[jump - 1], recv_k.at[jump - 1],
            "head", likes[jump - 1],
        )
    for jump in range(1, pairs):
        w_all[jump].wait_recv()
        slot = wout_ref.at[lax.rem(at_h + size_h - 2 * jump, size_h)]
        w_out[jump] = send(slot, slot, wsend_o.at[jump], wrecv_o.at[jump], "head", partner)
    total = p_like[...].astype(f32)
    for jump in range(1, pairs):
        like_sent[jump].wait_recv()
        total += r_like[jump - 1].astype(f32)
    out_ref[low_bit] = total.astype(out_ref.dtype)
    last = send(out_ref.at[low_bit], out_ref.at[low_bit], send_o, recv_o, "head", partner)
    for copy in w_out.values():
        copy.wait_recv()
    last.wait_recv()
    last.wait_send()
    for sent in (
        low_sent, ctx_sent, batch_sent, like_sent, w_low_sent, w_like_sent, w_all, w_out
    ):
        for copy in sent.values():
            copy.wait_send()


def sum_grads(values, wide, number):
    size_a, size_b, size_h = (lax.axis_size(axis) for axis in ("batch", "ctx", "head"))
    pairs = size_h // 2
    block, wide_block = values.shape[3:], wide.shape[1:]
    kind = values.dtype
    dma = pltpu.SemaphoreType.DMA
    vmem = pl.BlockSpec(memory_space=pltpu.VMEM)
    return pl.pallas_call(
        grads_kernel,
        out_shape=(
            jax.ShapeDtypeStruct((2,) + block, kind),
            jax.ShapeDtypeStruct(wide.shape, kind),
        ),
        in_specs=[vmem, vmem],
        out_specs=(vmem, vmem),
        scratch_shapes=[
            pltpu.VMEM((size_a, size_b) + block, kind),
            pltpu.VMEM((size_a, size_b - 1) + block, kind),
            pltpu.VMEM((size_a, size_b - 1) + block, kind),
            pltpu.VMEM((size_a - 1,) + block, kind),
            pltpu.VMEM((size_a - 1,) + block, kind),
            pltpu.VMEM(block, kind),
            pltpu.VMEM((pairs - 1,) + block, kind),
            pltpu.VMEM((pairs,) + wide_block, kind),
            pltpu.VMEM((pairs - 1,) + wide_block, kind),
            pltpu.VMEM((pairs - 1,) + wide_block, kind),
        ]
        + [dma((size_a, size_b))] * 2
        + [dma((size_a, size_b - 1))] * 2
        + [dma((size_a - 1,))] * 2
        + [dma((pairs - 1,))] * 2
        + [dma] * 2
        + [dma((pairs,))] * 2
        + [dma((pairs - 1,))] * 4
        + [dma((pairs,))] * 2,
        compiler_params=pltpu.CompilerParams(
            collective_id=number, has_side_effects=True, vmem_limit_bytes=vmem_limit
        ),
        name="sum_grads",
    )(values, wide)


def local(
    tokens,
    attn_in_gain,
    query_weight,
    key_weight,
    value_weight,
    query_gain,
    key_gain,
    out_weight,
    attn_out_gain,
    ffn_in_gain,
    gate_weight,
    up_weight,
    down_weight,
    ffn_out_gain,
    cotangent,
):
    low = jnp.bfloat16
    size_b, size_c, size_h = (lax.axis_size(axis) for axis in ("batch", "ctx", "head"))
    ctx_index = lax.axis_index("ctx")
    head_index = lax.axis_index("head")
    tok, width = tokens.shape[1:]
    head_dim = key_gain.shape[0]
    n_q, n_k, n_o = query_weight.shape[1], key_weight.shape[1], out_weight.shape[0]
    shards = size_b * size_c
    heads = n_q * shards // head_dim
    scale = head_dim ** (-0.5)

    packed = jnp.concatenate([query_weight.T, key_weight.T, value_weight.T, out_weight], axis=0)
    packed = jnp.pad(packed, ((0, -packed.shape[0] % (16 * size_h)), (0, 0)))
    full = gather_weights(packed.reshape(size_h, -1, width), 0).reshape(shards, -1, width)
    full_q = full[:, :n_q].reshape(-1, width)
    full_k = full[:, n_q : n_q + n_k].reshape(-1, width)
    full_v = full[:, n_q + n_k : n_q + 2 * n_k].reshape(-1, width)
    full_o = full[:, n_q + 2 * n_k : n_q + 2 * n_k + n_o].reshape(-1, width)

    inputs = tokens[0].astype(jnp.float32)
    first_pos = (ctx_index * size_h + head_index) * tok
    query_pos = first_pos + jnp.arange(tok, dtype=jnp.int32)
    cosine, sine = angles(query_pos.astype(jnp.float32), head_dim)
    normed_f, pull_in = jax.vjp(rms_scale, inputs, attn_in_gain)
    normed_in = normed_f.astype(low)
    query_raw = contract_cols(normed_in, full_q).reshape(tok, heads, head_dim)
    key_raw = contract_cols(normed_in, full_k)
    value_low = contract_cols(normed_in, full_v).astype(low)

    def query_path(values, gain):
        return rotate(rms_scale(values, gain), cosine[:, None, :], sine[:, None, :])

    def key_path(values, gain):
        return rotate(rms_scale(values, gain), cosine, sine)

    query_rot, pull_query = jax.vjp(query_path, query_raw, query_gain)
    key_rot, pull_key = jax.vjp(key_path, key_raw, key_gain)
    key_low = key_rot.astype(low)
    rows = heads * tok
    query_rows = query_rot.astype(low).transpose(1, 0, 2).reshape(rows, head_dim)
    pairs = gather(jnp.concatenate([key_low, value_low], axis=1), "ctx", "head", 1)
    pairs = pairs.reshape(-1, 2 * head_dim)
    key_rows, value_rows = pairs[:, :head_dim], pairs[:, head_dim:]
    length = key_rows.shape[0]

    scores = contract_cols(query_rows, key_rows) * scale
    key_pos = jnp.arange(length, dtype=jnp.int32)
    row_pos = jnp.tile(query_pos, heads)
    scores = jnp.where(key_pos[None, :] <= row_pos[:, None], scores, -jnp.inf)
    row_max = jnp.max(scores, axis=1, keepdims=True)
    raised = jnp.exp(scores - row_max)
    probs = raised * (1.0 / jnp.sum(raised, axis=1, keepdims=True))
    probs_low = probs.astype(low)
    attended = jnp.dot(probs_low, value_rows, preferred_element_type=jnp.float32)

    def to_tokens(values):
        return values.reshape(heads, tok, head_dim).transpose(1, 0, 2).reshape(tok, -1)

    attended_tok = to_tokens(attended.astype(low))
    projected = jnp.dot(attended_tok, full_o, preferred_element_type=jnp.float32)
    post_attn, pull_aout = jax.vjp(rms_scale, projected, attn_out_gain)
    resid = inputs + post_attn
    normed_ffn_f, pull_fin = jax.vjp(rms_scale, resid, ffn_in_gain)
    group_ffn = gather(normed_ffn_f.astype(low), "batch", "ctx", 2).reshape(-1, width)
    gate_pre = jnp.dot(group_ffn, gate_weight, preferred_element_type=jnp.float32)
    up_pre = jnp.dot(group_ffn, up_weight, preferred_element_type=jnp.float32)
    hidden_f, pull_glu = jax.vjp(geglu, gate_pre, up_pre)
    hidden = hidden_f.astype(low)
    mixed_part = jnp.dot(hidden, down_weight, preferred_element_type=jnp.float32).astype(low)
    mixed = scatter_sum(mixed_part.reshape(size_b, size_c, tok, width), "batch", "ctx", 3)
    post_ffn, pull_fout = jax.vjp(rms_scale, mixed, ffn_out_gain)
    block_out = (resid + post_ffn).astype(low)

    out_grad = cotangent[0].astype(jnp.float32)
    mixed_grad_f, fout_gain_grad = pull_fout(out_grad)
    mixed_grad = gather(mixed_grad_f.astype(low), "batch", "ctx", 4).reshape(-1, width)
    hidden_grad = contract_cols(mixed_grad, down_weight)
    gate_grad_f, up_grad_f = pull_glu(hidden_grad)
    gate_grad = gate_grad_f.astype(low)
    up_grad = up_grad_f.astype(low)
    ffn_part = (contract_cols(gate_grad, gate_weight) + contract_cols(up_grad, up_weight)).astype(
        low
    )
    normed_ffn_grad = scatter_sum(ffn_part.reshape(size_b, size_c, tok, width), "batch", "ctx", 5)
    down_grad = contract_rows(hidden, mixed_grad).astype(low)
    gate_w_grad = contract_rows(gate_grad, group_ffn).astype(low)
    up_w_grad = contract_rows(up_grad, group_ffn).astype(low)
    resid_part, fin_gain_grad = pull_fin(normed_ffn_grad)
    resid_grad = out_grad + resid_part
    projected_grad_f, aout_gain_grad = pull_aout(resid_grad)
    projected_grad = projected_grad_f.astype(low)
    out_w_grad = contract_rows(attended_tok, projected_grad).astype(low)
    attended_grad = contract_cols(projected_grad, full_o).astype(low)
    grad_rows = attended_grad.reshape(tok, heads, head_dim).transpose(1, 0, 2).reshape(rows, head_dim)
    delta = jnp.sum(grad_rows.astype(jnp.float32) * attended, axis=1)

    probs_grad = contract_cols(grad_rows, value_rows)
    score_grad = (probs * (probs_grad - delta[:, None])).astype(low)
    query_low_grad = jnp.dot(score_grad, key_rows, preferred_element_type=jnp.float32) * scale
    key_part = contract_rows(score_grad, query_rows) * scale
    value_part = contract_rows(probs_low, grad_rows)
    pair_part = jnp.concatenate([key_part.astype(low), value_part.astype(low)], axis=1)
    pair_grad = scatter_sum(
        pair_part.reshape(size_c, size_h, tok, 2 * head_dim), "ctx", "head", 6
    )
    key_low_grad, value_grad = pair_grad[:, :head_dim], pair_grad[:, head_dim:].astype(low)
    query_low_grad = to_tokens(query_low_grad.astype(low)).reshape(tok, heads, head_dim)
    query_raw_grad_f, query_gain_grad = pull_query(query_low_grad.astype(jnp.float32))
    key_raw_grad_f, key_gain_grad = pull_key(key_low_grad)
    query_raw_grad = query_raw_grad_f.reshape(tok, heads * head_dim).astype(low)
    key_raw_grad = key_raw_grad_f.astype(low)
    query_w_grad = contract_rows(query_raw_grad, normed_in).astype(low)
    key_w_grad = contract_rows(key_raw_grad, normed_in).astype(low)
    value_w_grad = contract_rows(value_grad, normed_in).astype(low)
    normed_in_grad = (
        jnp.dot(query_raw_grad, full_q, preferred_element_type=jnp.float32)
        + jnp.dot(key_raw_grad, full_k, preferred_element_type=jnp.float32)
        + jnp.dot(value_grad, full_v, preferred_element_type=jnp.float32)
    )
    inputs_part, ain_gain_grad = pull_in(normed_in_grad)
    inputs_grad = resid_grad + inputs_part

    gains = (
        ain_gain_grad,
        query_gain_grad,
        key_gain_grad,
        aout_gain_grad,
        fin_gain_grad,
        fout_gain_grad,
    )
    gain_flat = jnp.concatenate(gains)
    gain_rows = -(-gain_flat.shape[0] // width)
    fixed = n_q + 2 * n_k + n_o
    gain_pad = gain_rows + -(fixed + gain_rows) % 32
    gain_block = jnp.pad(gain_flat, (0, gain_pad * width - gain_flat.shape[0])).astype(low)
    gain_block = jnp.broadcast_to(gain_block.reshape(1, gain_pad, width), (shards, gain_pad, width))
    split = (
        query_w_grad.reshape(shards, n_q, width),
        key_w_grad.reshape(shards, n_k, width),
        value_w_grad.reshape(shards, n_k, width),
        out_w_grad.reshape(shards, n_o, width),
        gain_block,
    )
    grads = jnp.concatenate(split, axis=1)
    wide = jnp.concatenate([gate_w_grad, up_w_grad, down_grad], axis=0)
    wide = jnp.pad(wide, ((0, -wide.shape[0] % (16 * size_h)), (0, 0)))
    done, wide_done = sum_grads(
        grads.reshape(size_b, size_c, 2, -1, width), wide.reshape(size_h, -1, width), 7
    )
    done = jnp.concatenate(
        [done.reshape(-1, width), wide_done.reshape(-1, width)], axis=0
    ).astype(jnp.float32)

    parts = []
    start = 0
    n_f = gate_weight.shape[1]
    for count in (n_q, n_k, n_k, n_o, gain_pad, n_f, n_f, n_f):
        parts.append(done[start : start + count])
        start += count
    gain_done = parts[4].reshape(-1)
    gain_out = []
    start = 0
    for gain in gains:
        gain_out.append(gain_done[start : start + gain.shape[0]])
        start += gain.shape[0]
    return (
        block_out[None],
        inputs_grad[None],
        gain_out[0],
        parts[0].T,
        parts[1].T,
        parts[2].T,
        gain_out[1],
        gain_out[2],
        parts[3],
        gain_out[3],
        gain_out[4],
        parts[5].T,
        parts[6].T,
        parts[7],
        gain_out[5],
    )


def solution(mesh):
    in_specs = (
        P("batch", ("ctx", "head"), None),
        P(),
        P(None, ("batch", "ctx")),
        P(None, ("batch", "ctx")),
        P(None, ("batch", "ctx")),
        P(),
        P(),
        P(("batch", "ctx"), None),
        P(),
        P(),
        P(None, ("batch", "ctx")),
        P(None, ("batch", "ctx")),
        P(("batch", "ctx"), None),
        P(),
        P("batch", ("ctx", "head"), None),
    )
    out_specs = (
        P("batch", ("ctx", "head"), None),
        P("batch", ("ctx", "head"), None),
        P(),
        P(None, ("batch", "ctx")),
        P(None, ("batch", "ctx")),
        P(None, ("batch", "ctx")),
        P(),
        P(),
        P(("batch", "ctx"), None),
        P(),
        P(),
        P(None, ("batch", "ctx")),
        P(None, ("batch", "ctx")),
        P(("batch", "ctx"), None),
        P(),
    )
    return jax.shard_map(local, mesh=mesh, in_specs=in_specs, out_specs=out_specs, check_vma=False)
```
